512 devices in a mesh: seq: 128 (over z, x, y_lo), head: 4 (over y_hi, core).
Axes of the slice: x: 4, y: 8 (y_hi: 2, y_lo: 4; y = y_hi * 4 + y_lo), z: 8, core: 2. Of those that a mesh axis runs over, the one named last changes fastest.
Arguments:
- queries: bfloat16 [32768, 2048], P(('seq', 'head')), may hold values from -70 to 70
- keys: bfloat16 [32768, 2048], P(('seq', 'head')), may hold values from -21 to 21
- values: bfloat16 [32768, 2048], P(('seq', 'head')), may hold values from -16 to 16
- cotangent: bfloat16 [32768, 2048], P(('seq', 'head')), may hold values from -16 to 16
Outputs:
- output: bfloat16 [32768, 2048], P(('seq', 'head'))
- query_grads: bfloat16 [32768, 2048], P(('seq', 'head'))
- key_grads: bfloat16 [32768, 2048], P(('seq', 'head'))
- value_grads: bfloat16 [32768, 2048], P(('seq', 'head'))
The draws below stay inside these ranges and needn't reach their ends.
All inputs are finite; a program needn't handle non-finite values.
Results may differ from the reference program's by a relative error of at most 0.011.
Values may be sent and summed in bfloat16 or wider, within the bound.
No kernel may reach another device: no remote copies, remote signals or barrier semaphores. Data moves between devices by JAX's collectives and lax.ppermute only.
A program may use at most 64 MiB of HBM per device.

```python
import math
import jax
import jax.numpy as jnp
from jax import lax

H = 16
DH = 128
BLOCK = 128
TOKENS = 32768


def mixed_field(first_key, shape):
    gauss = jax.random.truncated_normal(first_key, -4.0, 4.0, shape, jnp.float32)
    return gauss


def layered(key, rows, cols):
    depth = max(rows.bit_length() - 1, 1)
    pieces = jax.random.split(key, 2 * depth + 2)
    base = mixed_field(pieces[0], (rows, cols))
    smooth = jnp.zeros((rows, cols), jnp.float32)
    for level in range(1, depth + 1):
        coarse = mixed_field(pieces[2 * level], (rows // 2 ** level, cols))
        smooth = smooth + jnp.repeat(coarse, 2 ** level, axis=0)
    return (base, smooth / math.sqrt(depth))


def draw_queries(key, part):
    key = jax.random.fold_in(key, 1)
    base, smooth = layered(key, TOKENS, H * DH)
    field = 1.6 * (0.8 * base + 0.6 * smooth)
    return field.astype(jnp.bfloat16)


def draw_keys(key, part):
    key = jax.random.fold_in(key, 2)
    base, smooth = layered(key, TOKENS, H * DH)
    field = 1.6 * (0.8 * base + 0.6 * smooth)
    return field.astype(jnp.bfloat16)


def draw_values(key, part):
    key = jax.random.fold_in(key, 3)
    base, smooth = layered(key, TOKENS, H * DH)
    field = 0.7 * (base + smooth)
    return field.astype(jnp.bfloat16)


def draw_cotangent(key, part):
    key = jax.random.fold_in(key, 4)
    base, smooth = layered(key, TOKENS, H * DH)
    field = 0.7 * (base + smooth)
    return field.astype(jnp.bfloat16)


def setup_inputs(seed: int = 0) -> dict:
    streams_of = jax.random.split(jax.random.key(seed), 5)
    queries = draw_queries(jax.random.fold_in(streams_of[4], 71), 0)
    keys = draw_keys(jax.random.fold_in(streams_of[4], 71), 0)
    values = draw_values(jax.random.fold_in(streams_of[4], 71), 0)
    cotangent = draw_cotangent(jax.random.fold_in(streams_of[4], 71), 0)
    return {"queries": queries, "keys": keys, "values": values, "cotangent": cotangent}


NEG_FILL = -1.0e30
LOG_TWO = math.log(2.0)


def halve_rows(x):
    pairs = x.reshape((x.shape[0] // 2, 2) + x.shape[1:]).astype(jnp.float32)
    return ((pairs[:, 0] + pairs[:, 1]) * 0.5).astype(jnp.bfloat16)


def spread_rows(grad):
    return jnp.repeat(grad * 0.5, 2, axis=0)


def flip_pairs(x):
    shaped = x.reshape((x.shape[0] // 2, 2) + x.shape[1:])
    return shaped[:, ::-1].reshape(x.shape)


def group_rows(x, groups):
    return x.reshape((groups, x.shape[0] // groups) + x.shape[1:])


def one_head(parts):
    query, key_in, value, grad_out = parts
    count = query.shape[0]
    blocks = count // BLOCK
    top_level = blocks.bit_length() - 2
    scale = DH ** -0.5
    pair = jnp.stack((key_in, value), 1)
    extended = jnp.pad(pair.reshape(blocks, BLOCK, 2, DH), ((1, 1), (0, 0), (0, 0), (0, 0)))
    window = jnp.concatenate((extended[:-2], extended[1:-1], extended[2:]), axis=1)
    lane = jnp.arange(3 * BLOCK) // BLOCK
    row_block = jnp.arange(blocks)
    left_gap = (row_block[:, None] == 0) & (lane[None, :] == 0)
    right_gap = (row_block[:, None] == blocks - 1) & (lane[None, :] == 2)
    allowed = jnp.logical_not(left_gap | right_gap)[:, None, :]
    levels = [(window, 0.0, allowed)]
    coarse = pair
    for level in range(1, top_level + 1):
        coarse = halve_rows(coarse)
        groups = count // (BLOCK * 2 ** level)
        levels.append((flip_pairs(group_rows(coarse, groups)), level * LOG_TWO, None))
    query_wide = query.astype(jnp.float32)
    grad_wide = grad_out.astype(jnp.float32)
    flat_scores = []
    for keyset, shift_by, allow in levels:
        groups = keyset.shape[0]
        score = jnp.einsum("gqd,gkd->gqk", group_rows(query_wide, groups), keyset[:, :, 0].astype(jnp.float32)) * scale + shift_by
        if allow is not None:
            score = jnp.where(allow, score, NEG_FILL)
        flat_scores.append(score.reshape(count, -1))
    row_max = flat_scores[0].max(axis=-1)
    for score in flat_scores[1:]:
        row_max = jnp.maximum(row_max, score.max(axis=-1))
    raised = [jnp.exp(score - row_max[:, None]) for score in flat_scores]
    total = jnp.sum(raised[0], axis=-1)
    for item in raised[1:]:
        total = total + jnp.sum(item, axis=-1)
    weights = [item / total[:, None] for item in raised]
    rounded = [item.astype(jnp.bfloat16) for item in weights]
    attended = jnp.zeros((count, DH), jnp.float32)
    for (keyset, shift_by, allow), light in zip(levels, rounded):
        groups = keyset.shape[0]
        attended = attended + jnp.einsum("gqk,gkd->gqd", group_rows(light.astype(jnp.float32), groups), keyset[:, :, 1].astype(jnp.float32)).reshape(count, DH)
    output = attended.astype(jnp.bfloat16)
    delta = jnp.sum(grad_wide * attended, axis=-1)
    query_grad = jnp.zeros((count, DH), jnp.float32)
    level_grads = []
    for (keyset, shift_by, allow), weight, light in zip(levels, weights, rounded):
        groups = keyset.shape[0]
        grouped_query = group_rows(query_wide, groups)
        grouped_grad = group_rows(grad_wide, groups)
        pushed = jnp.einsum("gqd,gkd->gqk", grouped_grad, keyset[:, :, 1].astype(jnp.float32))
        score_grad = (group_rows(weight, groups) * (pushed - group_rows(delta, groups)[..., None]) * scale).astype(jnp.bfloat16)
        score_wide = score_grad.astype(jnp.float32)
        query_grad = query_grad + jnp.einsum("gqk,gkd->gqd", score_wide, keyset[:, :, 0].astype(jnp.float32)).reshape(count, DH)
        key_grad = jnp.einsum("gqk,gqd->gkd", score_wide, grouped_query)
        value_grad = jnp.einsum("gqk,gqd->gkd", group_rows(light.astype(jnp.float32), groups), grouped_grad)
        level_grads.append(jnp.stack((key_grad, value_grad), 2))
    near = level_grads[0]
    padding = ((0, 0), (0, 0), (0, 0))
    spread_back = jnp.pad(near[:, :BLOCK], ((0, 2),) + padding) + jnp.pad(near[:, BLOCK:2 * BLOCK], ((1, 1),) + padding) + jnp.pad(near[:, 2 * BLOCK:], ((2, 0),) + padding)
    interior = spread_back[1:-1].reshape(count, 2, DH)
    down = None
    for level in range(top_level, 0, -1):
        direct = flip_pairs(level_grads[level]).reshape(count // 2 ** level, 2, DH)
        down = direct if down is None else spread_rows(down) + direct
    grads_pair = interior + spread_rows(down)
    return output, query_grad.astype(jnp.bfloat16), grads_pair[:, 0].astype(jnp.bfloat16), grads_pair[:, 1].astype(jnp.bfloat16)


def split_heads(x):
    return x.reshape(TOKENS, H, DH).transpose(1, 0, 2)


def join_heads(x):
    return x.transpose(1, 0, 2).reshape(TOKENS, H * DH)


def reference(queries, keys, values, cotangent):
    results = lax.map(one_head, (split_heads(queries), split_heads(keys), split_heads(values), split_heads(cotangent)))
    return (join_heads(results[0]), join_heads(results[1]), join_heads(results[2]), join_heads(results[3]))
```

```python
import functools
import math

import jax
import jax.numpy as jnp
from jax import lax
from jax.experimental import pallas as pl
from jax.experimental.pallas import tpu as pltpu
from jax.sharding import Mesh, PartitionSpec as P

DH = 128
BLOCK = 128
HEADS = 16
TOKENS_IN = 64
TOKENS = 1024
BLOCKS = TOKENS // BLOCK
RANKS = 32
CHUNK = 32
NEG_FILL = -1e30
SCALE = DH ** (-0.5)
SCALE_2 = SCALE * math.log2(math.e)
AXES = ("z", "x", "y_lo", "y_hi", "core")
HEAD_AXES = ("y_lo", "y_hi", "core")
SEQ_AXES = ("z", "x")
BF = jnp.bfloat16
F32 = jnp.float32
VMEM_LIMIT = 56 * 1024 * 1024

NN = (((1,), (0,)), ((), ()))
NT = (((1,), (1,)), ((), ()))


def dot(a, b, dims=NN):
    return lax.dot_general(a, b, dims, preferred_element_type=F32)


def eye(n):
    row = lax.broadcasted_iota(jnp.int32, (n, n), 0)
    col = lax.broadcasted_iota(jnp.int32, (n, n), 1)
    return jnp.where(row == col, 1.0, 0.0).astype(BF)


def kernel_call(body, outs, scratch=(), smem=False, n_in=1, flops=0, bytes_accessed=0):
    specs = [pl.BlockSpec(memory_space=pltpu.VMEM)] * n_in
    if smem:
        specs = [pl.BlockSpec(memory_space=pltpu.SMEM)] + specs
    return pl.pallas_call(
        body,
        out_shape=outs,
        in_specs=specs,
        out_specs=jax.tree.map(lambda _: pl.BlockSpec(memory_space=pltpu.VMEM), outs),
        scratch_shapes=list(scratch),
        compiler_params=pltpu.CompilerParams(vmem_limit_bytes=VMEM_LIMIT),
        cost_estimate=pl.CostEstimate(
            flops=flops, bytes_accessed=bytes_accessed, transcendentals=0
        ),
    )


def shape(*dims, dtype=BF):
    return jax.ShapeDtypeStruct(dims, dtype)


def pack_body(q_ref, k_ref, v_ref, d_ref, out_ref):
    for h in range(HEADS):
        for i, ref in enumerate((q_ref, k_ref, v_ref, d_ref)):
            out_ref[h, i] = ref[:, h * DH : (h + 1) * DH]


def unpack_body(in_ref, o_ref, dq_ref, dk_ref, dv_ref):
    for h in range(HEADS):
        for i, ref in enumerate((o_ref, dq_ref, dk_ref, dv_ref)):
            ref[:, h * DH : (h + 1) * DH] = in_ref[h, i]


def rows_of(ref, i, start, count):
    per = TOKENS_IN
    return ref[start // per : (start + count) // per, i].reshape(count, DH)


def pad_rows(x, rows):
    if x.shape[0] == rows:
        return x
    return jnp.concatenate([x, jnp.zeros((rows - x.shape[0], DH), x.dtype)], axis=0)


def pyramid_body(place_ref, in_ref, pyr_ref, zx_ref, p1_ref, p2_ref, p3_ref, p4_ref, buf):
    s = place_ref[0]
    odd = lax.rem(s, 2)
    for i in range(2):
        buf[...] = in_ref[:, 1 + i].reshape(TOKENS, DH).astype(F32)
        count = TOKENS
        levels = {}
        for level in range(1, 8):
            count //= 2
            mean = (
                (buf[pl.ds(0, count, stride=2), :] + buf[pl.ds(1, count, stride=2), :]) * 0.5
            ).astype(BF)
            mean = mean.astype(F32)
            levels[level] = mean
            if level < 7:
                buf[0:count, :] = mean
        pyr_ref[i, 0:512] = levels[1].astype(BF)
        pyr_ref[i, 512:768] = levels[2].astype(BF)
        p1_ref[i, 0:128] = levels[3].astype(BF)
        p2_ref[i] = levels[4].astype(BF)
        p3_ref[i, 0:64] = levels[4].astype(BF)
        for bit, level in ((2, 5), (3, 6), (4, 7)):
            rows = pad_rows(levels[level], CHUNK).astype(BF)
            for d in range(1 << bit, 2 << bit):
                zx_ref[jnp.bitwise_xor(s, d), i] = rows
        for d in range(4):
            zx_ref[jnp.bitwise_xor(s, d), i] = jnp.zeros((CHUNK, DH), BF)
        first = in_ref[0:2, 1 + i].reshape(BLOCK, DH)
        last = in_ref[14:16, 1 + i].reshape(BLOCK, DH)
        near = jnp.where(odd == 1, first, last)
        other = jnp.where(odd == 1, last, first)
        p1_ref[i, 128:256] = near
        p3_ref[i, 64:192] = other
        p4_ref[i] = other


def attend_body(
    place_ref,
    in_ref,
    pyr_ref,
    zx_ref,
    p1_ref,
    p2_ref,
    p3_ref,
    p4_ref,
    out_ref,
    dkv_ref,
    bzx_ref,
    b1_ref,
    b2_ref,
    b3_ref,
    b4_ref,
    win,
    rem,
    win_t,
    pyr_t,
    rem_t,
    dwin,
    dpyr,
    drem,
    spread,
):
    s = place_ref[0]
    x = lax.rem(s, 4)
    odd = lax.rem(s, 2) == 1
    inner = jnp.logical_or(x == 1, x == 2)
    ident = eye(DH)
    for i in range(2):
        near = p1_ref[i, 128:256]
        other = jnp.where(inner, p3_ref[i, 64:192], p4_ref[i])
        win[i, 0:128] = jnp.where(odd, near, other)
        win[i, 128:1152] = in_ref[:, 1 + i].reshape(TOKENS, DH)
        win[i, 1152:1280] = jnp.where(odd, other, near)
        rem[i, 0:128] = p1_ref[i, 0:128]
        rem[i, 128:192] = p2_ref[i]
        rem[i, 192:256] = p3_ref[i, 0:64]
        for bit, base in ((2, 256), (3, 384), (4, 512)):
            rows = BLOCK >> bit
            parts = []
            for d in range(1 << bit, 2 << bit):
                parts.append(zx_ref[jnp.bitwise_xor(s, d), i].astype(F32)[0:rows])
            rem[i, base : base + 128] = jnp.concatenate(parts, axis=0).astype(BF)
        win_t[i] = dot(ident, win[i], NT).astype(BF)
        pyr_t[i] = dot(ident, pyr_ref[i], NT).astype(BF)
        rem_t[i] = dot(ident, rem[i], NT).astype(BF)
    dwin[...] = jnp.zeros_like(dwin)
    drem[...] = jnp.zeros_like(drem)
    dpyr[...] = jnp.zeros_like(dpyr)
    left_bias = jnp.where(s == 0, NEG_FILL, 0.0).astype(F32)
    right_bias = jnp.where(s == RANKS - 1, NEG_FILL, 0.0).astype(F32)
    row = lax.broadcasted_iota(jnp.int32, (640, 1), 0)
    rem_shift = (row // BLOCK + 3).astype(F32)
    ident2 = eye(2 * BLOCK)
    for p in range(BLOCKS // 2):
        q = in_ref[4 * p : 4 * p + 4, 0].reshape(2 * BLOCK, DH)
        dy = in_ref[4 * p : 4 * p + 4, 3].reshape(2 * BLOCK, DH)
        one = (p ^ 1) * BLOCK
        two = 512 + ((p // 2) ^ 1) * BLOCK
        wide = (
            (pyr_ref, pyr_t, dpyr, one, BLOCK, 1.0),
            (pyr_ref, pyr_t, dpyr, two, BLOCK, 2.0),
            (rem, rem_t, drem, 0, 640, rem_shift),
        )
        score = []
        for ref, _, _, start, count, shift in wide:
            score.append(dot(ref[0, start : start + count], q, NT) * SCALE_2 + shift)
        fine = []
        for j in range(2):
            b = 2 * p + j
            f = dot(win[0, b * BLOCK : (b + 3) * BLOCK], q[j * BLOCK : (j + 1) * BLOCK], NT)
            f = f * SCALE_2
            if b == 0:
                f = jnp.concatenate([f[0:BLOCK] + left_bias, f[BLOCK:]], axis=0)
            if b == BLOCKS - 1:
                f = jnp.concatenate([f[: 2 * BLOCK], f[2 * BLOCK :] + right_bias], axis=0)
            fine.append(f)
        top = jnp.concatenate([jnp.max(f, axis=0, keepdims=True) for f in fine], axis=1)
        for item in score:
            top = jnp.maximum(top, jnp.max(item, axis=0, keepdims=True))
        score = [jnp.exp2(item - top) for item in score]
        fine = [
            jnp.exp2(f - top[:, j * BLOCK : (j + 1) * BLOCK]) for j, f in enumerate(fine)
        ]
        total = jnp.concatenate([jnp.sum(f, axis=0, keepdims=True) for f in fine], axis=1)
        for item in score:
            total = total + jnp.sum(item, axis=0, keepdims=True)
        inverse = 1.0 / total
        score = [item * inverse for item in score]
        fine = [f * inverse[:, j * BLOCK : (j + 1) * BLOCK] for j, f in enumerate(fine)]
        light = [item.astype(BF) for item in score]
        fine_light = [f.astype(BF) for f in fine]
        out_t = jnp.concatenate(
            [
                dot(win_t[1, :, (2 * p + j) * BLOCK : (2 * p + j + 3) * BLOCK], fine_light[j])
                for j in range(2)
            ],
            axis=1,
        )
        for (_, ref_t, _, start, count, _), item in zip(wide, light):
            out_t = out_t + dot(ref_t[1, :, start : start + count], item)
        dy_t = dot(ident, dy, NT)
        delta = jnp.sum(out_t * dy_t, axis=0, keepdims=True)
        out_ref[4 * p : 4 * p + 4, 0] = (
            dot(ident2, out_t.astype(BF), NT).astype(BF).reshape(4, TOKENS_IN, DH)
        )
        dq_t = []
        for j in range(2):
            b = 2 * p + j
            lanes = slice(j * BLOCK, (j + 1) * BLOCK)
            rows = slice(b * BLOCK, (b + 3) * BLOCK)
            pushed = dot(win[1, rows], dy[lanes], NT)
            grad = (fine[j] * ((pushed - delta[:, lanes]) * SCALE)).astype(BF)
            dq_t.append(dot(win_t[0, :, rows], grad))
            dwin[0, rows] += dot(grad, q[lanes])
            dwin[1, rows] += dot(fine_light[j], dy[lanes])
        dq_t = jnp.concatenate(dq_t, axis=1)
        for (ref, ref_t, dref, start, count, _), item, item_light in zip(wide, score, light):
            rows = slice(start, start + count)
            pushed = dot(ref[1, rows], dy, NT)
            grad = (item * ((pushed - delta) * SCALE)).astype(BF)
            dq_t = dq_t + dot(ref_t[0, :, rows], grad)
            dref[0, rows] += dot(grad, q)
            dref[1, rows] += dot(item_light, dy)
        out_ref[4 * p : 4 * p + 4, 1] = (
            dot(ident2, dq_t.astype(BF), NT).astype(BF).reshape(4, TOKENS_IN, DH)
        )
    for i in range(2):
        half = dpyr[i, 512:768] * 0.5
        spread[pl.ds(0, 256, stride=2), :] = half
        spread[pl.ds(1, 256, stride=2), :] = half
        half = (dpyr[i, 0:512] + spread[0:512, :]) * 0.5
        spread[pl.ds(0, 512, stride=2), :] = half
        spread[pl.ds(1, 512, stride=2), :] = half
        dkv_ref[i] = dwin[i, 128:1152] + spread[...]
        left = dwin[i, 0:128].astype(BF)
        right = dwin[i, 1152:1280].astype(BF)
        near = jnp.where(odd, left, right)
        other = jnp.where(odd, right, left)
        b1_ref[i, 0:128] = drem[i, 0:128].astype(BF)
        b1_ref[i, 128:256] = near
        b2_ref[i] = drem[i, 128:192].astype(BF)
        b3_ref[i, 0:64] = drem[i, 192:256].astype(BF)
        b3_ref[i, 64:192] = other
        b4_ref[i] = other
        for d in range(4):
            bzx_ref[jnp.bitwise_xor(s, d), i] = jnp.zeros((CHUNK, DH), BF)
        for bit, base in ((2, 256), (3, 384), (4, 512)):
            rows = BLOCK >> bit
            for d in range(1 << bit, 2 << bit):
                start = base + (d - (1 << bit)) * rows
                bzx_ref[jnp.bitwise_xor(s, d), i] = pad_rows(
                    drem[i, start : start + rows], CHUNK
                ).astype(BF)


def finish_body(
    place_ref, out_ref_in, dkv_ref, zx_ref, p1_ref, p2_ref, p3_ref, p4_ref, out_ref, spread
):
    s = place_ref[0]
    x = lax.rem(s, 4)
    odd = lax.rem(s, 2) == 1
    inner = jnp.logical_or(x == 1, x == 2)
    out_ref[:, 0:2] = out_ref_in[...]
    for i in range(2):
        direct = {
            3: p1_ref[i, 0:128].astype(F32),
            4: p2_ref[i].astype(F32) + p3_ref[i, 0:64].astype(F32),
        }
        for bit in (2, 3, 4):
            total = None
            for d in range(1 << bit, 2 << bit):
                item = zx_ref[jnp.bitwise_xor(s, d), i].astype(F32)
                total = item if total is None else total + item
            direct[bit + 3] = total[0 : BLOCK >> bit]
        carry = direct[7]
        for level in range(6, 2, -1):
            count = carry.shape[0]
            half = carry * 0.5
            spread[pl.ds(0, count, stride=2), :] = half
            spread[pl.ds(1, count, stride=2), :] = half
            carry = direct[level] + spread[0 : 2 * count, :]
        for _ in range(3):
            count = carry.shape[0]
            half = carry * 0.5
            spread[pl.ds(0, count, stride=2), :] = half
            spread[pl.ds(1, count, stride=2), :] = half
            carry = spread[0 : 2 * count, :]
        near = p1_ref[i, 128:256].astype(F32)
        other = jnp.where(inner, p3_ref[i, 64:192], p4_ref[i]).astype(F32)
        first = jnp.where(odd, near, other)
        last = jnp.where(odd, other, near)
        grad = dkv_ref[i] + carry
        grad = jnp.concatenate(
            [grad[0:128] + first, grad[128 : TOKENS - 128], grad[TOKENS - 128 :] + last], axis=0
        )
        out_ref[:, 2 + i] = grad.astype(BF).reshape(HEADS, TOKENS_IN, DH)


def swap(array, axes):
    return lax.all_to_all(array, axes, split_axis=0, concat_axis=0, tiled=True)


def cross_pairs(z_count, x_count):
    pairs = []
    for z in range(z_count - 1):
        low, high = z * x_count + x_count - 1, (z + 1) * x_count
        pairs += [(low, high), (high, low)]
    return pairs


def exchange(zx, p1, p2, p3, p4):
    flip = lambda array, mask: lax.ppermute(array, "x", [(i, i ^ mask) for i in range(4)])
    p1 = flip(p1, 1)
    p3 = flip(p3, 3)
    p2 = flip(p2, 2)
    p4 = lax.ppermute(p4, SEQ_AXES, cross_pairs(8, 4))
    return swap(zx, SEQ_AXES), p1, p2, p3, p4


def on_device(queries, keys, values, cotangent):
    place = (lax.axis_index("z") * 4 + lax.axis_index("x")).reshape(1).astype(jnp.int32)
    mb = 1 << 20
    messages = [
        shape(RANKS, 2, CHUNK, DH),
        shape(2, 256, DH),
        shape(2, 64, DH),
        shape(2, 192, DH),
        shape(2, 128, DH),
    ]
    packed = kernel_call(
        pack_body, shape(HEADS, 4, TOKENS_IN, DH), n_in=4, bytes_accessed=2 * mb
    )(queries, keys, values, cotangent)
    mine = swap(packed, HEAD_AXES)
    pyr, *sent = kernel_call(
        pyramid_body,
        [shape(2, 768, DH)] + messages,
        scratch=[pltpu.VMEM((TOKENS, DH), F32)],
        smem=True,
        n_in=1,
        bytes_accessed=2 * mb,
    )(place, mine)
    got = exchange(*sent)
    out, dkv, *back = kernel_call(
        attend_body,
        [shape(HEADS, 2, TOKENS_IN, DH), shape(2, TOKENS, DH, dtype=F32)] + messages,
        scratch=[
            pltpu.VMEM((2, 1280, DH), BF),
            pltpu.VMEM((2, 640, DH), BF),
            pltpu.VMEM((2, DH, 1280), BF),
            pltpu.VMEM((2, DH, 768), BF),
            pltpu.VMEM((2, DH, 640), BF),
            pltpu.VMEM((2, 1280, DH), F32),
            pltpu.VMEM((2, 768, DH), F32),
            pltpu.VMEM((2, 640, DH), F32),
            pltpu.VMEM((TOKENS, DH), F32),
        ],
        smem=True,
        n_in=7,
        flops=2 * 10**9,
        bytes_accessed=5 * mb,
    )(place, mine, pyr, *got)
    returned = exchange(*back)
    packed = kernel_call(
        finish_body,
        shape(HEADS, 4, TOKENS_IN, DH),
        scratch=[pltpu.VMEM((TOKENS, DH), F32)],
        smem=True,
        n_in=7,
        bytes_accessed=3 * mb,
    )(place, out, dkv, *returned)
    results = swap(packed, HEAD_AXES)
    flat = shape(TOKENS_IN, HEADS * DH)
    return tuple(
        kernel_call(unpack_body, [flat] * 4, n_in=1, bytes_accessed=2 * mb)(results)
    )


def solution(mesh):
    fine = Mesh(mesh.devices.reshape(8, 4, 4, 2, 2), AXES)
    placed = P(AXES, None)
    return jax.shard_map(
        on_device,
        mesh=fine,
        in_specs=(placed,) * 4,
        out_specs=(placed,) * 4,
        check_vma=False,
    )
```

```python
import functools
import math

import jax
import jax.numpy as jnp
from jax import lax
from jax.experimental import pallas as pl
from jax.experimental.pallas import tpu as pltpu
from jax.sharding import Mesh, PartitionSpec as P

DH = 128
BLOCK = 128
HEADS = 16
TOKENS_IN = 64
TOKENS = 1024
BLOCKS = TOKENS // BLOCK
RANKS = 32
CHUNK = 32
NEG_FILL = -1e30
SCALE = DH ** (-0.5)
SCALE_2 = SCALE * math.log2(math.e)
AXES = ("z", "x", "y_lo", "y_hi", "core")
HEAD_AXES = ("y_lo", "y_hi", "core")
SEQ_AXES = ("z", "x")
BF = jnp.bfloat16
F32 = jnp.float32
SMALL, MIDDLE, LARGE = 4, 16, 56
VMEM, HBM, SMEM = pltpu.VMEM, pltpu.HBM, pltpu.SMEM

NN = (((1,), (0,)), ((), ()))
NT = (((1,), (1,)), ((), ()))


def dot(a, b, dims=NN):
    return lax.dot_general(a, b, dims, preferred_element_type=F32)


def eye(n):
    row = lax.broadcasted_iota(jnp.int32, (n, n), 0)
    col = lax.broadcasted_iota(jnp.int32, (n, n), 1)
    return jnp.where(row == col, 1.0, 0.0).astype(BF)


def kernel_call(body, ins, outs, scratch=(), flops=0, bytes_accessed=0, mib=SMALL):
    space = lambda kind: pl.BlockSpec(memory_space=kind)
    many = len(outs) > 1
    return pl.pallas_call(
        body,
        out_shape=[item for _, item in outs] if many else outs[0][1],
        in_specs=[space(kind) for kind in ins],
        out_specs=[space(kind) for kind, _ in outs] if many else space(outs[0][0]),
        scratch_shapes=list(scratch),
        compiler_params=pltpu.CompilerParams(vmem_limit_bytes=mib << 20),
        cost_estimate=pl.CostEstimate(
            flops=flops, bytes_accessed=bytes_accessed, transcendentals=0
        ),
    )


def shape(*dims, dtype=BF):
    return jax.ShapeDtypeStruct(dims, dtype)


def pack_body(q_ref, k_ref, v_ref, d_ref, out_ref, held, packed, in_sem, out_sem):
    refs = (q_ref, k_ref, v_ref, d_ref)
    loads = [pltpu.make_async_copy(ref, held.at[i], in_sem.at[i]) for i, ref in enumerate(refs)]
    stores = [
        pltpu.make_async_copy(packed.at[i], out_ref.at[:, i], out_sem.at[i]) for i in range(4)
    ]
    for load in loads:
        load.start()
    for i in range(4):
        loads[i].wait()
        for h in range(HEADS):
            packed[i, h] = held[i, :, h * DH : (h + 1) * DH]
        stores[i].start()
    for store in stores:
        store.wait()


def unpack_body(in_ref, o_ref, dq_ref, dk_ref, dv_ref):
    for h in range(HEADS):
        for i, ref in enumerate((o_ref, dq_ref, dk_ref, dv_ref)):
            ref[:, h * DH : (h + 1) * DH] = in_ref[h, i]


def rows_of(ref, i, start, count):
    per = TOKENS_IN
    return ref[start // per : (start + count) // per, i].reshape(count, DH)


def pad_rows(x, rows):
    if x.shape[0] == rows:
        return x
    return jnp.concatenate([x, jnp.zeros((rows - x.shape[0], DH), x.dtype)], axis=0)


def pyramid_body(place_ref, in_ref, pyr_ref, zx_ref, p1_ref, p2_ref, p3_ref, p4_ref, buf):
    s = place_ref[0]
    odd = lax.rem(s, 2)
    for i in range(2):
        buf[...] = in_ref[:, 1 + i].reshape(TOKENS, DH).astype(F32)
        count = TOKENS
        levels = {}
        for level in range(1, 8):
            count //= 2
            mean = (
                (buf[pl.ds(0, count, stride=2), :] + buf[pl.ds(1, count, stride=2), :]) * 0.5
            ).astype(BF)
            mean = mean.astype(F32)
            levels[level] = mean
            if level < 7:
                buf[0:count, :] = mean
        pyr_ref[i, 0:512] = levels[1].astype(BF)
        pyr_ref[i, 512:768] = levels[2].astype(BF)
        p1_ref[i, 0:128] = levels[3].astype(BF)
        p2_ref[i] = levels[4].astype(BF)
        p3_ref[i] = levels[4].astype(BF)
        for bit, level in ((2, 5), (3, 6), (4, 7)):
            rows = pad_rows(levels[level], CHUNK).astype(BF)
            for d in range(1 << bit, 2 << bit):
                zx_ref[jnp.bitwise_xor(s, d), i] = rows
        for d in range(4):
            zx_ref[jnp.bitwise_xor(s, d), i] = jnp.zeros((CHUNK, DH), BF)
        first = in_ref[0:2, 1 + i].reshape(BLOCK, DH)
        last = in_ref[14:16, 1 + i].reshape(BLOCK, DH)
        near = jnp.where(odd == 1, first, last)
        other = jnp.where(odd == 1, last, first)
        p1_ref[i, 128:256] = near
        p4_ref[i] = other


def merge_body(place_ref, zx_ref, p1_ref, p2_ref, p3_ref, p4_ref, rem_ref, edge_ref):
    s = place_ref[0]
    odd = lax.rem(s, 2) == 1
    for i in range(2):
        near = p1_ref[i, 128:256]
        other = p4_ref[i]
        edge_ref[i, 0:128] = jnp.where(odd, near, other)
        edge_ref[i, 128:256] = jnp.where(odd, other, near)
        rem_ref[i, 0:128] = p1_ref[i, 0:128]
        rem_ref[i, 128:192] = p2_ref[i]
        rem_ref[i, 192:256] = p3_ref[i]
        for bit, base in ((2, 256), (3, 384), (4, 512)):
            rows = BLOCK >> bit
            parts = []
            for d in range(1 << bit, 2 << bit):
                parts.append(zx_ref[jnp.bitwise_xor(s, d), i].astype(F32)[0:rows])
            rem_ref[i, base : base + 128] = jnp.concatenate(parts, axis=0).astype(BF)


def part_body(place_ref, drem_ref, dedge_ref, bzx_ref, b1_ref, b2_ref, b3_ref, b4_ref):
    s = place_ref[0]
    odd = lax.rem(s, 2) == 1
    for i in range(2):
        left = dedge_ref[i, 0:128]
        right = dedge_ref[i, 128:256]
        b1_ref[i, 0:128] = drem_ref[i, 0:128]
        b1_ref[i, 128:256] = jnp.where(odd, left, right)
        b2_ref[i] = drem_ref[i, 128:192]
        b3_ref[i] = drem_ref[i, 192:256]
        b4_ref[i] = jnp.where(odd, right, left)
        for d in range(4):
            bzx_ref[jnp.bitwise_xor(s, d), i] = jnp.zeros((CHUNK, DH), BF)
        for bit, base in ((2, 256), (3, 384), (4, 512)):
            rows = BLOCK >> bit
            block = drem_ref[i, base : base + 128].astype(F32)
            for d in range(1 << bit, 2 << bit):
                start = (d - (1 << bit)) * rows
                bzx_ref[jnp.bitwise_xor(s, d), i] = pad_rows(
                    block[start : start + rows], CHUNK
                ).astype(BF)


def attend_body(
    place_ref,
    in_ref,
    pyr_ref,
    rem,
    edge_ref,
    out_ref,
    dkv_ref,
    drem_ref,
    dedge_ref,
    win,
    win_t,
    pyr_t,
    rem_t,
    dwin,
    dpyr,
    drem,
    spread,
):
    s = place_ref[0]
    ident = eye(DH)
    for i in range(2):
        win[i, 0:128] = edge_ref[i, 0:128]
        win[i, 128:1152] = in_ref[:, 1 + i].reshape(TOKENS, DH)
        win[i, 1152:1280] = edge_ref[i, 128:256]
        win_t[i] = dot(ident, win[i], NT).astype(BF)
        pyr_t[i] = dot(ident, pyr_ref[i], NT).astype(BF)
        rem_t[i] = dot(ident, rem[i], NT).astype(BF)
    dwin[...] = jnp.zeros_like(dwin)
    drem[...] = jnp.zeros_like(drem)
    dpyr[...] = jnp.zeros_like(dpyr)
    second = lax.broadcasted_iota(jnp.int32, (1, 2 * BLOCK), 1) >= BLOCK
    ident2 = eye(2 * BLOCK)

    def load(p):
        q = in_ref[4 * p : 4 * p + 4, 0].reshape(2 * BLOCK, DH)
        dy = in_ref[4 * p : 4 * p + 4, 3].reshape(2 * BLOCK, DH)
        one = (p ^ 1) * BLOCK
        two = 512 + ((p // 2) ^ 1) * BLOCK
        groups = (
            (win, win_t, dwin, 2 * p * BLOCK, (0, 0, 0, 0)),
            (pyr_ref, pyr_t, dpyr, one, (1,)),
            (pyr_ref, pyr_t, dpyr, two, (2,)),
            (rem, rem_t, drem, 0, (3, 4, 5, 6, 7)),
        )
        raws = [dot(ref[0, start : start + BLOCK * len(shifts)], q, NT) for ref, _, _, start, shifts in groups]
        pushes = [dot(ref[1, start : start + BLOCK * len(shifts)], dy, NT) for ref, _, _, start, shifts in groups] if True else None
        dy_t = dot(ident, dy, NT)
        return q, dy, groups, raws, pushes, dy_t
    def soft(p, state):
        q, dy, groups, raws, pushes, dy_t = state
        first_gap = jnp.where(second, NEG_FILL, 0.0).astype(F32)
        last_gap = jnp.where(second, 0.0, NEG_FILL).astype(F32)
        if p == 0:
            first_gap = jnp.where(s == 0, NEG_FILL, first_gap)
        if p == BLOCKS // 2 - 1:
            last_gap = jnp.where(s == RANKS - 1, NEG_FILL, last_gap)
        score = []
        top = None
        for raw, (ref, _, _, start, shifts) in zip(raws, groups):
            blocks = [raw[n * BLOCK : (n + 1) * BLOCK] for n in range(len(shifts))]
            if len(shifts) == 4:
                blocks[0] = blocks[0] + first_gap
                blocks[3] = blocks[3] + last_gap
            for item, shift in zip(blocks, shifts):
                peak = jnp.max(item, axis=0, keepdims=True) * SCALE_2 + float(shift)
                top = peak if top is None else jnp.maximum(top, peak)
            score.append(blocks)
        total = jnp.zeros((1, 2 * BLOCK), F32)
        for blocks, group in zip(score, groups):
            for n, shift in enumerate(group[4]):
                blocks[n] = jnp.exp2(blocks[n] * SCALE_2 + (float(shift) - top))
                total = total + jnp.sum(blocks[n], axis=0, keepdims=True)
        inverse = 1.0 / total
        score = [jnp.concatenate(blocks, axis=0) * inverse for blocks in score]
        light = [item.astype(BF) for item in score]
        return score, light
    def tail(p, state, weights):
        q, dy, groups, raws, pushes, dy_t = state
        score, light = weights
        out_t = jnp.zeros((DH, 2 * BLOCK), F32)
        for (_, ref_t, _, start, shifts), item in zip(groups, light):
            out_t = out_t + dot(ref_t[1, :, start : start + BLOCK * len(shifts)], item)
        delta = jnp.sum(out_t * dy_t, axis=0, keepdims=True)
        out_ref[4 * p : 4 * p + 4, 0] = (
            dot(ident2, out_t.astype(BF), NT).astype(BF).reshape(4, TOKENS_IN, DH)
        )
        dq_t = jnp.zeros((DH, 2 * BLOCK), F32)
        for n, ((ref, ref_t, dref, start, shifts), item, item_light) in enumerate(zip(groups, score, light)):
            rows = slice(start, start + BLOCK * len(shifts))
            pushed = pushes[n] if True else dot(ref[1, rows], dy, NT)
            grad = (item * (pushed - delta)).astype(BF)
            dq_t = dq_t + dot(ref_t[0, :, rows], grad)
            dref[0, rows] += dot(grad, q)
            dref[1, rows] += dot(item_light, dy)
        out_ref[4 * p : 4 * p + 4, 1] = (
            dot(ident2, (dq_t * SCALE).astype(BF), NT).astype(BF).reshape(4, TOKENS_IN, DH)
        )
    state = load(0)
    weights = soft(0, state)
    for p in range(4):
        following = load(p + 1) if p < 3 else None
        after = soft(p + 1, following) if p < 3 else None
        tail(p, state, weights)
        state, weights = following, after
    dwin[0] = dwin[0] * SCALE
    dpyr[0] = dpyr[0] * SCALE
    drem[0] = drem[0] * SCALE
    for i in range(2):
        drem_ref[i] = drem[i].astype(BF)
        dedge_ref[i, 0:128] = dwin[i, 0:128].astype(BF)
        dedge_ref[i, 128:256] = dwin[i, 1152:1280].astype(BF)
        half = dpyr[i, 512:768] * 0.5
        spread[pl.ds(0, 256, stride=2), :] = half
        spread[pl.ds(1, 256, stride=2), :] = half
        half = (dpyr[i, 0:512] + spread[0:512, :]) * 0.5
        spread[pl.ds(0, 512, stride=2), :] = half
        spread[pl.ds(1, 512, stride=2), :] = half
        dkv_ref[i] = dwin[i, 128:1152] + spread[...]


def finish_body(
    place_ref, out_ref_in, dkv_ref, zx_ref, p1_ref, p2_ref, p3_ref, p4_ref, out_ref, spread
):
    s = place_ref[0]
    odd = lax.rem(s, 2) == 1
    out_ref[:, 0:2] = out_ref_in[...]
    for i in range(2):
        direct = {
            3: p1_ref[i, 0:128].astype(F32),
            4: p2_ref[i].astype(F32) + p3_ref[i].astype(F32),
        }
        for bit in (2, 3, 4):
            total = None
            for d in range(1 << bit, 2 << bit):
                item = zx_ref[jnp.bitwise_xor(s, d), i].astype(F32)
                total = item if total is None else total + item
            direct[bit + 3] = total[0 : BLOCK >> bit]
        carry = direct[7]
        for level in range(6, 2, -1):
            count = carry.shape[0]
            half = carry * 0.5
            spread[pl.ds(0, count, stride=2), :] = half
            spread[pl.ds(1, count, stride=2), :] = half
            carry = direct[level] + spread[0 : 2 * count, :]
        for _ in range(3):
            count = carry.shape[0]
            half = carry * 0.5
            spread[pl.ds(0, count, stride=2), :] = half
            spread[pl.ds(1, count, stride=2), :] = half
            carry = spread[0 : 2 * count, :]
        near = p1_ref[i, 128:256].astype(F32)
        other = p4_ref[i].astype(F32)
        first = jnp.where(odd, near, other)
        last = jnp.where(odd, other, near)
        grad = dkv_ref[i] + carry
        grad = jnp.concatenate(
            [grad[0:128] + first, grad[128 : TOKENS - 128], grad[TOKENS - 128 :] + last], axis=0
        )
        out_ref[:, 2 + i] = grad.astype(BF).reshape(HEADS, TOKENS_IN, DH)


def swap(array, axes):
    return lax.all_to_all(array, axes, split_axis=0, concat_axis=0, tiled=True)


def odd_pairs(count):
    pairs = []
    for low in range(1, count - 1, 2):
        pairs += [(low, low + 1), (low + 1, low)]
    return pairs


def exchange(zx, p1, p2, p3, p4):
    flip = lambda array, mask: lax.ppermute(array, "x", [(i, i ^ mask) for i in range(4)])
    p1 = flip(p1, 1)
    p2 = flip(p2, 2)
    p3 = flip(p3, 3)
    p4 = lax.ppermute(p4, SEQ_AXES, odd_pairs(RANKS))
    return swap(zx, SEQ_AXES), p1, p2, p3, p4


def on_device(queries, keys, values, cotangent):
    place = (lax.axis_index("z") * 4 + lax.axis_index("x")).reshape(1).astype(jnp.int32)
    mb = 1 << 20
    messages = [
        shape(RANKS, 2, CHUNK, DH),
        shape(2, 256, DH),
        shape(2, 64, DH),
        shape(2, 64, DH),
        shape(2, 128, DH),
    ]
    split = shape(HEADS, 4, TOKENS_IN, DH)
    packed = kernel_call(
        pack_body,
        [HBM] * 4,
        [(HBM, split)],
        scratch=[
            VMEM((4, TOKENS_IN, HEADS * DH), BF),
            VMEM((4, HEADS, TOKENS_IN, DH), BF),
            pltpu.SemaphoreType.DMA((4,)),
            pltpu.SemaphoreType.DMA((4,)),
        ],
        mib=LARGE,
        bytes_accessed=2 * mb,
    )(queries, keys, values, cotangent)
    mine = swap(packed, HEAD_AXES)
    pyr, *sent = kernel_call(
        pyramid_body,
        [SMEM, VMEM],
        [(VMEM, shape(2, 768, DH))] + [(VMEM, item) for item in messages],
        scratch=[VMEM((TOKENS, DH), F32)],
        bytes_accessed=2 * mb,
    )(place, mine)
    got = exchange(*sent)
    rows = [shape(2, 640, DH), shape(2, 256, DH)]
    far = kernel_call(merge_body, [SMEM] + [VMEM] * 5, [(VMEM, item) for item in rows])(
        place, *got
    )
    out, dkv, *grads = kernel_call(
        attend_body,
        [SMEM] + [VMEM] * 4,
        [
            (VMEM, shape(HEADS, 2, TOKENS_IN, DH)),
            (VMEM, shape(2, TOKENS, DH, dtype=F32)),
        ]
        + [(VMEM, item) for item in rows],
        scratch=[
            VMEM((2, 1280, DH), BF),
            VMEM((2, DH, 1280), BF),
            VMEM((2, DH, 768), BF),
            VMEM((2, DH, 640), BF),
            VMEM((2, 1280, DH), F32),
            VMEM((2, 768, DH), F32),
            VMEM((2, 640, DH), F32),
            VMEM((TOKENS, DH), F32),
        ],
        mib=MIDDLE,
        flops=2 * 10**9,
        bytes_accessed=5 * mb,
    )(place, mine, pyr, *far)
    back = kernel_call(part_body, [SMEM] + [VMEM] * 2, [(VMEM, item) for item in messages])(
        place, *grads
    )
    returned = exchange(*back)
    packed = kernel_call(
        finish_body,
        [SMEM] + [VMEM] * 7,
        [(VMEM, split)],
        scratch=[VMEM((TOKENS, DH), F32)],
        bytes_accessed=3 * mb,
    )(place, out, dkv, *returned)
    results = swap(packed, HEAD_AXES)
    flat = shape(TOKENS_IN, HEADS * DH)
    return tuple(
        kernel_call(unpack_body, [VMEM], [(VMEM, flat)] * 4, bytes_accessed=2 * mb)(results)
    )


def solution(mesh):
    fine = Mesh(mesh.devices.reshape(8, 4, 4, 2, 2), AXES)
    placed = P(AXES, None)
    return jax.shard_map(
        on_device,
        mesh=fine,
        in_specs=(placed,) * 4,
        out_specs=(placed,) * 4,
        check_vma=False,
    )
```

```python
import functools
import math

import jax
import jax.numpy as jnp
from jax import lax
from jax.experimental import pallas as pl
from jax.experimental.pallas import tpu as pltpu
from jax.sharding import Mesh, PartitionSpec as P

DH = 128
BLOCK = 128
HEADS = 16
TOKENS_IN = 64
TOKENS = 1024
BLOCKS = TOKENS // BLOCK
RANKS = 32
CHUNK = 32
NEG_FILL = -1e30
SCALE = DH ** (-0.5)
SCALE_2 = SCALE * math.log2(math.e)
AXES = ("z", "x", "y_lo", "y_hi", "core")
HEAD_AXES = ("y_lo", "y_hi", "core")
SEQ_AXES = ("z", "x")
BF = jnp.bfloat16
F32 = jnp.float32
SMALL, MIDDLE, LARGE = 4, 16, 56
VMEM, HBM, SMEM = pltpu.VMEM, pltpu.HBM, pltpu.SMEM

NN = (((1,), (0,)), ((), ()))
NT = (((1,), (1,)), ((), ()))
TN = (((0,), (0,)), ((), ()))


def dot(a, b, dims=NN):
    return lax.dot_general(a, b, dims, preferred_element_type=F32)


def kernel_call(body, ins, outs, scratch=(), flops=0, bytes_accessed=0, mib=SMALL):
    space = lambda kind: pl.BlockSpec(memory_space=kind)
    many = len(outs) > 1
    return pl.pallas_call(
        body,
        out_shape=[item for _, item in outs] if many else outs[0][1],
        in_specs=[space(kind) for kind in ins],
        out_specs=[space(kind) for kind, _ in outs] if many else space(outs[0][0]),
        scratch_shapes=list(scratch),
        compiler_params=pltpu.CompilerParams(vmem_limit_bytes=mib << 20),
        cost_estimate=pl.CostEstimate(
            flops=flops, bytes_accessed=bytes_accessed, transcendentals=0
        ),
    )


def shape(*dims, dtype=BF):
    return jax.ShapeDtypeStruct(dims, dtype)


def pack_body(q_ref, k_ref, v_ref, d_ref, out_ref, held, packed, in_sem, out_sem):
    refs = (q_ref, k_ref, v_ref, d_ref)
    loads = [pltpu.make_async_copy(ref, held.at[i], in_sem.at[i]) for i, ref in enumerate(refs)]
    stores = [
        pltpu.make_async_copy(packed.at[i], out_ref.at[:, i], out_sem.at[i]) for i in range(4)
    ]
    for load in loads:
        load.start()
    for i in range(4):
        loads[i].wait()
        for h in range(HEADS):
            packed[i, h] = held[i, :, h * DH : (h + 1) * DH]
        stores[i].start()
    for store in stores:
        store.wait()


def unpack_body(in_ref, o_ref, dq_ref, dk_ref, dv_ref, held, out_sem):
    refs = (o_ref, dq_ref, dk_ref, dv_ref)
    stores = [pltpu.make_async_copy(held.at[i], ref, out_sem.at[i]) for i, ref in enumerate(refs)]
    for i in range(4):
        for h in range(HEADS):
            held[i, :, h * DH : (h + 1) * DH] = in_ref[h, i]
        stores[i].start()
    for store in stores:
        store.wait()


def rows_of(ref, i, start, count):
    per = TOKENS_IN
    return ref[start // per : (start + count) // per, i].reshape(count, DH)


def pad_rows(x, rows):
    if x.shape[0] == rows:
        return x
    return jnp.concatenate([x, jnp.zeros((rows - x.shape[0], DH), x.dtype)], axis=0)


def pyramid_body(place_ref, in_ref, pyr_ref, zx_ref, p1_ref, p2_ref, p3_ref, p4_ref, buf):
    s = place_ref[0]
    odd = lax.rem(s, 2)
    for i in range(2):
        buf[...] = in_ref[:, 1 + i].reshape(TOKENS, DH).astype(F32)
        count = TOKENS
        levels = {}
        for level in range(1, 8):
            count //= 2
            mean = (
                (buf[pl.ds(0, count, stride=2), :] + buf[pl.ds(1, count, stride=2), :]) * 0.5
            ).astype(BF)
            mean = mean.astype(F32)
            levels[level] = mean
            if level < 7:
                buf[0:count, :] = mean
        pyr_ref[i, 0:512] = levels[1].astype(BF)
        pyr_ref[i, 512:768] = levels[2].astype(BF)
        p1_ref[i, 0:128] = levels[3].astype(BF)
        p2_ref[i] = levels[4].astype(BF)
        p3_ref[i] = levels[4].astype(BF)
        for bit, level in ((2, 5), (3, 6), (4, 7)):
            rows = pad_rows(levels[level], CHUNK).astype(BF)
            for d in range(1 << bit, 2 << bit):
                zx_ref[jnp.bitwise_xor(s, d), i] = rows
        for d in range(4):
            zx_ref[jnp.bitwise_xor(s, d), i] = jnp.zeros((CHUNK, DH), BF)
        first = in_ref[0:2, 1 + i].reshape(BLOCK, DH)
        last = in_ref[14:16, 1 + i].reshape(BLOCK, DH)
        near = jnp.where(odd == 1, first, last)
        other = jnp.where(odd == 1, last, first)
        p1_ref[i, 128:256] = near
        p4_ref[i] = other


def merge_body(place_ref, zx_ref, p1_ref, p2_ref, p3_ref, p4_ref, rem_ref, edge_ref):
    s = place_ref[0]
    odd = lax.rem(s, 2) == 1
    for i in range(2):
        near = p1_ref[i, 128:256]
        other = p4_ref[i]
        edge_ref[i, 0:128] = jnp.where(odd, near, other)
        edge_ref[i, 128:256] = jnp.where(odd, other, near)
        rem_ref[i, 0:128] = p1_ref[i, 0:128]
        rem_ref[i, 128:192] = p2_ref[i]
        rem_ref[i, 192:256] = p3_ref[i]
        for bit, base in ((2, 256), (3, 384), (4, 512)):
            rows = BLOCK >> bit
            parts = []
            for d in range(1 << bit, 2 << bit):
                parts.append(zx_ref[jnp.bitwise_xor(s, d), i].astype(F32)[0:rows])
            rem_ref[i, base : base + 128] = jnp.concatenate(parts, axis=0).astype(BF)


def part_body(place_ref, drem_ref, dedge_ref, bzx_ref, b1_ref, b2_ref, b3_ref, b4_ref):
    s = place_ref[0]
    odd = lax.rem(s, 2) == 1
    for i in range(2):
        left = dedge_ref[i, 0:128]
        right = dedge_ref[i, 128:256]
        b1_ref[i, 0:128] = drem_ref[i, 0:128]
        b1_ref[i, 128:256] = jnp.where(odd, left, right)
        b2_ref[i] = drem_ref[i, 128:192]
        b3_ref[i] = drem_ref[i, 192:256]
        b4_ref[i] = jnp.where(odd, right, left)
        for d in range(4):
            bzx_ref[jnp.bitwise_xor(s, d), i] = jnp.zeros((CHUNK, DH), BF)
        for bit, base in ((2, 256), (3, 384), (4, 512)):
            rows = BLOCK >> bit
            block = drem_ref[i, base : base + 128].astype(F32)
            for d in range(1 << bit, 2 << bit):
                start = (d - (1 << bit)) * rows
                bzx_ref[jnp.bitwise_xor(s, d), i] = pad_rows(
                    block[start : start + rows], CHUNK
                ).astype(BF)


def attend_body(
    place_ref,
    in_ref,
    pyr_ref,
    rem,
    edge_ref,
    out_ref,
    dkv_ref,
    drem_ref,
    dedge_ref,
    win,
    dwin,
    dpyr,
    drem,
    spread,
):
    s = place_ref[0]
    for i in range(2):
        win[i, 0:128] = edge_ref[i, 0:128]
        win[i, 128:1152] = in_ref[:, 1 + i].reshape(TOKENS, DH)
        win[i, 1152:1280] = edge_ref[i, 128:256]
    dwin[...] = jnp.zeros_like(dwin)
    drem[...] = jnp.zeros_like(drem)
    dpyr[...] = jnp.zeros_like(dpyr)
    second = lax.broadcasted_iota(jnp.int32, (1, 2 * BLOCK), 1) >= BLOCK

    def products(p):
        q = in_ref[4 * p : 4 * p + 4, 0].reshape(2 * BLOCK, DH)
        dy = in_ref[4 * p : 4 * p + 4, 3].reshape(2 * BLOCK, DH)
        one = (p ^ 1) * BLOCK
        two = 512 + ((p // 2) ^ 1) * BLOCK
        groups = (
            (win, dwin, slice(2 * p * BLOCK, (2 * p + 4) * BLOCK), (0, 0, 0, 0)),
            (pyr_ref, dpyr, slice(one, one + BLOCK), (1,)),
            (pyr_ref, dpyr, slice(two, two + BLOCK), (2,)),
            (rem, drem, slice(0, 640), (3, 4, 5, 6, 7)),
        )
        raws = [dot(ref[0, rows], q, NT) for ref, _, rows, _ in groups]
        pushes = [dot(ref[1, rows], dy, NT) for ref, _, rows, _ in groups]
        return q, dy, groups, raws, pushes

    def softmax(p, state):
        _, _, groups, raws, _ = state
        first_gap = jnp.where(second, NEG_FILL, 0.0).astype(F32)
        last_gap = jnp.where(second, 0.0, NEG_FILL).astype(F32)
        if p == 0:
            first_gap = jnp.where(s == 0, NEG_FILL, first_gap)
        if p == BLOCKS // 2 - 1:
            last_gap = jnp.where(s == RANKS - 1, NEG_FILL, last_gap)
        score = []
        top = None
        for raw, (_, _, _, shifts) in zip(raws, groups):
            blocks = [raw[n * BLOCK : (n + 1) * BLOCK] for n in range(len(shifts))]
            if len(shifts) == 4:
                blocks[0] = blocks[0] + first_gap
                blocks[3] = blocks[3] + last_gap
            for item, shift in zip(blocks, shifts):
                peak = jnp.max(item, axis=0, keepdims=True) * SCALE_2 + float(shift)
                top = peak if top is None else jnp.maximum(top, peak)
            score.append(blocks)
        total = jnp.zeros((1, 2 * BLOCK), F32)
        for blocks, (_, _, _, shifts) in zip(score, groups):
            for n, shift in enumerate(shifts):
                blocks[n] = jnp.exp2(blocks[n] * SCALE_2 + (float(shift) - top))
                total = total + jnp.sum(blocks[n], axis=0, keepdims=True)
        inverse = 1.0 / total
        score = [jnp.concatenate(blocks, axis=0) * inverse for blocks in score]
        return score, [item.astype(BF) for item in score]

    def gradients(p, state, weights):
        q, dy, groups, _, pushes = state
        score, light = weights
        slots = slice(4 * p, 4 * p + 4)
        tall = None
        for item, pushed in zip(score, pushes):
            for n in range(0, item.shape[0], BLOCK):
                term = item[n : n + BLOCK] * pushed[n : n + BLOCK]
                tall = term if tall is None else tall + term
        delta = jnp.sum(tall, axis=0, keepdims=True)
        out = jnp.zeros((2 * BLOCK, DH), F32)
        dq = jnp.zeros((2 * BLOCK, DH), F32)
        for (ref, dref, rows, _), item, item_light, pushed in zip(groups, score, light, pushes):
            out = out + dot(item_light, ref[1, rows], TN)
            grad = (item * (pushed - delta)).astype(BF)
            dq = dq + dot(grad, ref[0, rows], TN)
            dref[0, rows] += dot(grad, q)
            dref[1, rows] += dot(item_light, dy)
        out_ref[slots, 0] = out.astype(BF).reshape(4, TOKENS_IN, DH)
        out_ref[slots, 1] = (dq * SCALE).astype(BF).reshape(4, TOKENS_IN, DH)

    state = products(0)
    weights = softmax(0, state)
    for p in range(BLOCKS // 2):
        last = p == BLOCKS // 2 - 1
        following = None if last else products(p + 1)
        after = None if last else softmax(p + 1, following)
        gradients(p, state, weights)
        state, weights = following, after
    dwin[0] = dwin[0] * SCALE
    dpyr[0] = dpyr[0] * SCALE
    drem[0] = drem[0] * SCALE
    for i in range(2):
        drem_ref[i] = drem[i].astype(BF)
        dedge_ref[i, 0:128] = dwin[i, 0:128].astype(BF)
        dedge_ref[i, 128:256] = dwin[i, 1152:1280].astype(BF)
        half = dpyr[i, 512:768] * 0.5
        spread[pl.ds(0, 256, stride=2), :] = half
        spread[pl.ds(1, 256, stride=2), :] = half
        half = (dpyr[i, 0:512] + spread[0:512, :]) * 0.5
        spread[pl.ds(0, 512, stride=2), :] = half
        spread[pl.ds(1, 512, stride=2), :] = half
        dkv_ref[i] = dwin[i, 128:1152] + spread[...]


def finish_body(
    place_ref, out_ref_in, dkv_ref, zx_ref, p1_ref, p2_ref, p3_ref, p4_ref, out_ref, spread
):
    s = place_ref[0]
    odd = lax.rem(s, 2) == 1
    out_ref[:, 0:2] = out_ref_in[...]
    for i in range(2):
        direct = {
            3: p1_ref[i, 0:128].astype(F32),
            4: p2_ref[i].astype(F32) + p3_ref[i].astype(F32),
        }
        for bit in (2, 3, 4):
            total = None
            for d in range(1 << bit, 2 << bit):
                item = zx_ref[jnp.bitwise_xor(s, d), i].astype(F32)
                total = item if total is None else total + item
            direct[bit + 3] = total[0 : BLOCK >> bit]
        carry = direct[7]
        for level in range(6, 2, -1):
            count = carry.shape[0]
            half = carry * 0.5
            spread[pl.ds(0, count, stride=2), :] = half
            spread[pl.ds(1, count, stride=2), :] = half
            carry = direct[level] + spread[0 : 2 * count, :]
        for _ in range(3):
            count = carry.shape[0]
            half = carry * 0.5
            spread[pl.ds(0, count, stride=2), :] = half
            spread[pl.ds(1, count, stride=2), :] = half
            carry = spread[0 : 2 * count, :]
        near = p1_ref[i, 128:256].astype(F32)
        other = p4_ref[i].astype(F32)
        first = jnp.where(odd, near, other)
        last = jnp.where(odd, other, near)
        grad = dkv_ref[i] + carry
        grad = jnp.concatenate(
            [grad[0:128] + first, grad[128 : TOKENS - 128], grad[TOKENS - 128 :] + last], axis=0
        )
        out_ref[:, 2 + i] = grad.astype(BF).reshape(HEADS, TOKENS_IN, DH)


def swap(array, axes):
    return lax.all_to_all(array, axes, split_axis=0, concat_axis=0, tiled=True)


def odd_pairs(count):
    pairs = []
    for low in range(1, count - 1, 2):
        pairs += [(low, low + 1), (low + 1, low)]
    return pairs


def exchange(zx, p1, p2, p3, p4):
    flip = lambda array, mask: lax.ppermute(array, "x", [(i, i ^ mask) for i in range(4)])
    p1 = flip(p1, 1)
    p2 = flip(p2, 2)
    p3 = flip(p3, 3)
    p4 = lax.ppermute(p4, SEQ_AXES, odd_pairs(RANKS))
    return swap(zx, SEQ_AXES), p1, p2, p3, p4


def on_device(queries, keys, values, cotangent):
    place = (lax.axis_index("z") * 4 + lax.axis_index("x")).reshape(1).astype(jnp.int32)
    mb = 1 << 20
    messages = [
        shape(RANKS, 2, CHUNK, DH),
        shape(2, 256, DH),
        shape(2, 64, DH),
        shape(2, 64, DH),
        shape(2, 128, DH),
    ]
    split = shape(HEADS, 4, TOKENS_IN, DH)
    packed = kernel_call(
        pack_body,
        [HBM] * 4,
        [(HBM, split)],
        scratch=[
            VMEM((4, TOKENS_IN, HEADS * DH), BF),
            VMEM((4, HEADS, TOKENS_IN, DH), BF),
            pltpu.SemaphoreType.DMA((4,)),
            pltpu.SemaphoreType.DMA((4,)),
        ],
        mib=LARGE,
        bytes_accessed=2 * mb,
    )(queries, keys, values, cotangent)
    mine = swap(packed, HEAD_AXES)
    pyr, *sent = kernel_call(
        pyramid_body,
        [SMEM, VMEM],
        [(VMEM, shape(2, 768, DH))] + [(VMEM, item) for item in messages],
        scratch=[VMEM((TOKENS, DH), F32)],
        bytes_accessed=2 * mb,
    )(place, mine)
    got = exchange(*sent)
    rows = [shape(2, 640, DH), shape(2, 256, DH)]
    far = kernel_call(merge_body, [SMEM] + [VMEM] * 5, [(VMEM, item) for item in rows])(
        place, *got
    )
    out, dkv, *grads = kernel_call(
        attend_body,
        [SMEM] + [VMEM] * 4,
        [
            (VMEM, shape(HEADS, 2, TOKENS_IN, DH)),
            (VMEM, shape(2, TOKENS, DH, dtype=F32)),
        ]
        + [(VMEM, item) for item in rows],
        scratch=[
            VMEM((2, 1280, DH), BF),
            VMEM((2, 1280, DH), F32),
            VMEM((2, 768, DH), F32),
            VMEM((2, 640, DH), F32),
            VMEM((TOKENS, DH), F32),
        ],
        mib=MIDDLE,
        flops=2 * 10**9,
        bytes_accessed=5 * mb,
    )(place, mine, pyr, *far)
    back = kernel_call(part_body, [SMEM] + [VMEM] * 2, [(VMEM, item) for item in messages])(
        place, *grads
    )
    returned = exchange(*back)
    packed = kernel_call(
        finish_body,
        [SMEM] + [VMEM] * 7,
        [(VMEM, split)],
        scratch=[VMEM((TOKENS, DH), F32)],
        bytes_accessed=3 * mb,
    )(place, out, dkv, *returned)
    results = swap(packed, HEAD_AXES)
    flat = shape(TOKENS_IN, HEADS * DH)
    return tuple(
        kernel_call(
            unpack_body,
            [VMEM],
            [(HBM, flat)] * 4,
            scratch=[VMEM((4, TOKENS_IN, HEADS * DH), BF), pltpu.SemaphoreType.DMA((4,))],
            bytes_accessed=2 * mb,
        )(results)
    )


def solution(mesh):
    fine = Mesh(mesh.devices.reshape(8, 4, 4, 2, 2), AXES)
    placed = P(AXES, None)
    return jax.shard_map(
        on_device,
        mesh=fine,
        in_specs=(placed,) * 4,
        out_specs=(placed,) * 4,
        check_vma=False,
    )
```

```python
import functools
import math

import jax
import jax.numpy as jnp
from jax import lax
from jax.experimental import pallas as pl
from jax.experimental.pallas import tpu as pltpu
from jax.sharding import Mesh, PartitionSpec as P

DH = 128
BLOCK = 128
HEADS = 16
TOKENS_IN = 64
TOKENS = 1024
BLOCKS = TOKENS // BLOCK
RANKS = 32
CHUNK = 32
NEG_FILL = -1e30
SCALE = DH ** (-0.5)
SCALE_2 = SCALE * math.log2(math.e)
AXES = ("z", "x", "y_lo", "y_hi", "core")
HEAD_AXES = ("y_lo", "y_hi", "core")
SEQ_AXES = ("z", "x")
BF = jnp.bfloat16
F32 = jnp.float32
SMALL, MIDDLE, LARGE = 4, 16, 56
VMEM, HBM, SMEM = pltpu.VMEM, pltpu.HBM, pltpu.SMEM

NN = (((1,), (0,)), ((), ()))
NT = (((1,), (1,)), ((), ()))
TN = (((0,), (0,)), ((), ()))


def dot(a, b, dims=NN):
    return lax.dot_general(a, b, dims, preferred_element_type=F32)


def kernel_call(body, ins, outs, scratch=(), flops=0, bytes_accessed=0, mib=SMALL):
    space = lambda kind: pl.BlockSpec(memory_space=kind)
    many = len(outs) > 1
    return pl.pallas_call(
        body,
        out_shape=[item for _, item in outs] if many else outs[0][1],
        in_specs=[space(kind) for kind in ins],
        out_specs=[space(kind) for kind, _ in outs] if many else space(outs[0][0]),
        scratch_shapes=list(scratch),
        compiler_params=pltpu.CompilerParams(vmem_limit_bytes=mib << 20),
        cost_estimate=pl.CostEstimate(
            flops=flops, bytes_accessed=bytes_accessed, transcendentals=0
        ),
    )


def shape(*dims, dtype=BF):
    return jax.ShapeDtypeStruct(dims, dtype)


def pack_body(a_ref, b_ref, out_ref, held, packed, in_sem, out_sem):
    refs = (a_ref, b_ref)
    loads = [pltpu.make_async_copy(ref, held.at[i], in_sem.at[i]) for i, ref in enumerate(refs)]
    stores = [
        pltpu.make_async_copy(packed.at[i], out_ref.at[:, i], out_sem.at[i]) for i in range(2)
    ]
    for load in loads:
        load.start()
    for i in range(2):
        loads[i].wait()
        for h in range(HEADS):
            packed[i, h] = held[i, :, h * DH : (h + 1) * DH]
        stores[i].start()
    for store in stores:
        store.wait()


def unpack_body(in_ref, o_ref, dq_ref, dk_ref, dv_ref, held, out_sem):
    refs = (o_ref, dq_ref, dk_ref, dv_ref)
    stores = [pltpu.make_async_copy(held.at[i], ref, out_sem.at[i]) for i, ref in enumerate(refs)]
    for i in range(4):
        for h in range(HEADS):
            held[i, :, h * DH : (h + 1) * DH] = in_ref[h, i]
        stores[i].start()
    for store in stores:
        store.wait()


def rows_of(ref, i, start, count):
    per = TOKENS_IN
    return ref[start // per : (start + count) // per, i].reshape(count, DH)


def pad_rows(x, rows):
    if x.shape[0] == rows:
        return x
    return jnp.concatenate([x, jnp.zeros((rows - x.shape[0], DH), x.dtype)], axis=0)


def pyramid_body(place_ref, in_ref, pyr_ref, z_ref, p1_ref, p2_ref, p4_ref, buf):
    s = place_ref[0]
    z = s // 4
    odd = lax.rem(s, 2)
    for i in range(2):
        buf[...] = in_ref[:, i].reshape(TOKENS, DH).astype(F32)
        count = TOKENS
        levels = {}
        for level in range(1, 8):
            count //= 2
            mean = (
                (buf[pl.ds(0, count, stride=2), :] + buf[pl.ds(1, count, stride=2), :]) * 0.5
            ).astype(BF)
            mean = mean.astype(F32)
            levels[level] = mean
            if level < 7:
                buf[0:count, :] = mean
        pyr_ref[i, 0:512] = levels[1].astype(BF)
        pyr_ref[i, 512:768] = levels[2].astype(BF)
        p1_ref[i, 0:128] = levels[3].astype(BF)
        p2_ref[i] = levels[4].astype(BF)
        z_ref[z, i] = jnp.zeros((CHUNK, DH), BF)
        for bit in range(3):
            rows = pad_rows(levels[5 + bit], CHUNK).astype(BF)
            for d in range(1 << bit, 2 << bit):
                z_ref[jnp.bitwise_xor(z, d), i] = rows
        first = in_ref[0:2, i].reshape(BLOCK, DH)
        last = in_ref[14:16, i].reshape(BLOCK, DH)
        p1_ref[i, 128:256] = jnp.where(odd == 1, first, last)
        p4_ref[i] = jnp.where(odd == 1, last, first)


def join_body(place_ref, z_ref, p1_ref, p2_ref, own_ref, out1_ref, out2_ref):
    z = place_ref[0] // 4
    for i in range(2):
        for bit in range(3):
            parts = [
                z_ref[jnp.bitwise_xor(z, d), i].astype(F32)[0 : CHUNK >> bit]
                for d in range(1 << bit, 2 << bit)
            ]
            rows = parts[0] if bit == 0 else jnp.concatenate(parts, axis=0)
            own_ref[i, bit * CHUNK : (bit + 1) * CHUNK] = rows.astype(BF)
        out1_ref[i, 0:256] = p1_ref[i]
        out1_ref[i, 256:352] = own_ref[i]
        out2_ref[i, 0:64] = p2_ref[i]
        out2_ref[i, 64:160] = own_ref[i]


def merge_body(place_ref, own_ref, p1_ref, p2_ref, p3_ref, p4_ref, rem_ref, edge_ref):
    odd = lax.rem(place_ref[0], 2) == 1
    for i in range(2):
        near = p1_ref[i, 128:256]
        other = p4_ref[i]
        edge_ref[i, 0:128] = jnp.where(odd, near, other)
        edge_ref[i, 128:256] = jnp.where(odd, other, near)
        rem_ref[i, 0:128] = p1_ref[i, 0:128]
        rem_ref[i, 128:192] = p2_ref[i, 0:64]
        rem_ref[i, 192:256] = p3_ref[i, 0:64]
        for e, (ref, base) in enumerate(((own_ref, 0), (p1_ref, 256), (p2_ref, 64), (p3_ref, 64))):
            for bit in range(3):
                start = 256 + bit * BLOCK + e * CHUNK
                rem_ref[i, start : start + CHUNK] = ref[
                    i, base + bit * CHUNK : base + (bit + 1) * CHUNK
                ]


def part_body(place_ref, drem_ref, dedge_ref, bzx_ref, b1_ref, b2_ref, b3_ref, b4_ref):
    s = place_ref[0]
    odd = lax.rem(s, 2) == 1
    for i in range(2):
        left = dedge_ref[i, 0:128]
        right = dedge_ref[i, 128:256]
        b1_ref[i, 0:128] = drem_ref[i, 0:128]
        b1_ref[i, 128:256] = jnp.where(odd, left, right)
        b2_ref[i] = drem_ref[i, 128:192]
        b3_ref[i] = drem_ref[i, 192:256]
        b4_ref[i] = jnp.where(odd, right, left)
        for d in range(4):
            bzx_ref[jnp.bitwise_xor(s, d), i] = jnp.zeros((CHUNK, DH), BF)
        for bit in range(3):
            count = CHUNK >> bit
            base = 256 + bit * BLOCK
            block = drem_ref[i, base : base + BLOCK].astype(F32)
            for d in range(1 << bit, 2 << bit):
                for e in range(4):
                    start = e * CHUNK + (d - (1 << bit)) * count
                    bzx_ref[jnp.bitwise_xor(s, 4 * d + e), i] = pad_rows(
                        block[start : start + count], CHUNK
                    ).astype(BF)


def attend_body(
    place_ref,
    kv_ref,
    qd_ref,
    pyr_ref,
    rem,
    edge_ref,
    out_ref,
    dkv_ref,
    drem_ref,
    dedge_ref,
    win,
    dwin,
    dpyr,
    drem,
    spread,
):
    s = place_ref[0]
    for i in range(2):
        win[i, 0:128] = edge_ref[i, 0:128]
        win[i, 128:1152] = kv_ref[:, i].reshape(TOKENS, DH)
        win[i, 1152:1280] = edge_ref[i, 128:256]
    written = set()

    def accumulate(ref, rows, key_grad, value_grad):
        for base in range(rows.start, rows.stop, BLOCK):
            block = slice(base, base + BLOCK)
            part = slice(base - rows.start, base - rows.start + BLOCK)
            for i, grad in enumerate((key_grad, value_grad)):
                if (id(ref), base) in written:
                    ref[i, block] += grad[part]
                else:
                    ref[i, block] = grad[part]
            written.add((id(ref), base))

    second = lax.broadcasted_iota(jnp.int32, (1, 2 * BLOCK), 1) >= BLOCK
    halves = (slice(0, BLOCK), slice(BLOCK, 2 * BLOCK))

    def products(p):
        q = qd_ref[4 * p : 4 * p + 4, 0].reshape(2 * BLOCK, DH)
        dy = qd_ref[4 * p : 4 * p + 4, 1].reshape(2 * BLOCK, DH)
        one = (p ^ 1) * BLOCK
        two = 512 + ((p // 2) ^ 1) * BLOCK
        outer = [slice((2 * p + n) * BLOCK, (2 * p + n + 1) * BLOCK) for n in (0, 3)]
        groups = (
            (win, dwin, slice((2 * p + 1) * BLOCK, (2 * p + 3) * BLOCK), (0, 0)),
            (pyr_ref, dpyr, slice(one, one + BLOCK), (1,)),
            (pyr_ref, dpyr, slice(two, two + BLOCK), (2,)),
            (rem, drem, slice(0, 640), (3, 4, 5, 6, 7)),
        )

        def scored(i, other):
            tiles = [dot(win[i, rows], other[half], NT) for rows, half in zip(outer, halves)]
            return [jnp.concatenate(tiles, axis=1)] + [
                dot(ref[i, rows], other, NT) for ref, _, rows, _ in groups
            ]

        return q, dy, outer, groups, scored(0, q), scored(1, dy)

    def softmax(p, state):
        _, _, _, groups, raws, _ = state
        raws = list(raws)
        if p == 0:
            raws[0] = raws[0] + jnp.where(
                jnp.logical_and(s == 0, jnp.logical_not(second)), NEG_FILL, 0.0
            ).astype(F32)
        if p == BLOCKS // 2 - 1:
            raws[0] = raws[0] + jnp.where(
                jnp.logical_and(s == RANKS - 1, second), NEG_FILL, 0.0
            ).astype(F32)
        score = []
        top = None
        every = [(0,)] + [shifts for _, _, _, shifts in groups]
        for raw, shifts in zip(raws, every):
            blocks = [raw[n * BLOCK : (n + 1) * BLOCK] for n in range(len(shifts))]
            for item, shift in zip(blocks, shifts):
                peak = jnp.max(item, axis=0, keepdims=True) * SCALE_2 + float(shift)
                top = peak if top is None else jnp.maximum(top, peak)
            score.append(blocks)
        total = jnp.zeros((1, 2 * BLOCK), F32)
        for blocks, shifts in zip(score, every):
            for n, shift in enumerate(shifts):
                blocks[n] = jnp.exp2(blocks[n] * SCALE_2 + (float(shift) - top))
                total = total + jnp.sum(blocks[n], axis=0, keepdims=True)
        inverse = 1.0 / total
        score = [jnp.concatenate(blocks, axis=0) * inverse for blocks in score]
        return score, [item.astype(BF) for item in score]

    def gradients(p, state, weights):
        q, dy, outer, groups, _, pushes = state
        score, light = weights
        slots = slice(4 * p, 4 * p + 4)
        tall = None
        for item, pushed in zip(score, pushes):
            for n in range(0, item.shape[0], BLOCK):
                term = item[n : n + BLOCK] * pushed[n : n + BLOCK]
                tall = term if tall is None else tall + term
        delta = jnp.sum(tall, axis=0, keepdims=True)
        grads = [(item * (pushed - delta)).astype(BF) for item, pushed in zip(score, pushes)]
        out = []
        dq = []
        for rows, half in zip(outer, halves):
            out.append(dot(light[0][:, half], win[1, rows], TN))
            dq.append(dot(grads[0][:, half], win[0, rows], TN))
            accumulate(
                dwin, rows, dot(grads[0][:, half], q[half]), dot(light[0][:, half], dy[half])
            )
        out = jnp.concatenate(out, axis=0)
        dq = jnp.concatenate(dq, axis=0)
        for (ref, dref, rows, _), item_light, grad in zip(groups, light[1:], grads[1:]):
            out = out + dot(item_light, ref[1, rows], TN)
            dq = dq + dot(grad, ref[0, rows], TN)
            accumulate(dref, rows, dot(grad, q), dot(item_light, dy))
        out_ref[slots, 0] = out.astype(BF).reshape(4, TOKENS_IN, DH)
        out_ref[slots, 1] = (dq * SCALE).astype(BF).reshape(4, TOKENS_IN, DH)

    state = products(0)
    weights = softmax(0, state)
    for p in range(BLOCKS // 2):
        last = p == BLOCKS // 2 - 1
        following = None if last else products(p + 1)
        after = None if last else softmax(p + 1, following)
        gradients(p, state, weights)
        state, weights = following, after
    dwin[0] = dwin[0] * SCALE
    dpyr[0] = dpyr[0] * SCALE
    drem[0] = drem[0] * SCALE
    for i in range(2):
        drem_ref[i] = drem[i].astype(BF)
        dedge_ref[i, 0:128] = dwin[i, 0:128].astype(BF)
        dedge_ref[i, 128:256] = dwin[i, 1152:1280].astype(BF)
        half = dpyr[i, 512:768] * 0.5
        spread[pl.ds(0, 256, stride=2), :] = half
        spread[pl.ds(1, 256, stride=2), :] = half
        half = (dpyr[i, 0:512] + spread[0:512, :]) * 0.5
        spread[pl.ds(0, 512, stride=2), :] = half
        spread[pl.ds(1, 512, stride=2), :] = half
        dkv_ref[i] = dwin[i, 128:1152] + spread[...]


def finish_body(
    place_ref, out_ref_in, dkv_ref, zx_ref, p1_ref, p2_ref, p3_ref, p4_ref, out_ref, spread
):
    s = place_ref[0]
    odd = lax.rem(s, 2) == 1
    out_ref[:, 0:2] = out_ref_in[...]
    for i in range(2):
        direct = {
            3: p1_ref[i, 0:128].astype(F32),
            4: p2_ref[i].astype(F32) + p3_ref[i].astype(F32),
        }
        for bit in (2, 3, 4):
            total = None
            for d in range(1 << bit, 2 << bit):
                item = zx_ref[jnp.bitwise_xor(s, d), i].astype(F32)
                total = item if total is None else total + item
            direct[bit + 3] = total[0 : BLOCK >> bit]
        carry = direct[7]
        for level in range(6, 2, -1):
            count = carry.shape[0]
            half = carry * 0.5
            spread[pl.ds(0, count, stride=2), :] = half
            spread[pl.ds(1, count, stride=2), :] = half
            carry = direct[level] + spread[0 : 2 * count, :]
        for _ in range(3):
            count = carry.shape[0]
            half = carry * 0.5
            spread[pl.ds(0, count, stride=2), :] = half
            spread[pl.ds(1, count, stride=2), :] = half
            carry = spread[0 : 2 * count, :]
        near = p1_ref[i, 128:256].astype(F32)
        other = p4_ref[i].astype(F32)
        first = jnp.where(odd, near, other)
        last = jnp.where(odd, other, near)
        grad = dkv_ref[i] + carry
        grad = jnp.concatenate(
            [grad[0:128] + first, grad[128 : TOKENS - 128], grad[TOKENS - 128 :] + last], axis=0
        )
        out_ref[:, 2 + i] = grad.astype(BF).reshape(HEADS, TOKENS_IN, DH)


def swap(array, axes):
    return lax.all_to_all(array, axes, split_axis=0, concat_axis=0, tiled=True)


def odd_pairs(count):
    pairs = []
    for low in range(1, count - 1, 2):
        pairs += [(low, low + 1), (low + 1, low)]
    return pairs


def flip(array, mask):
    return lax.ppermute(array, "x", [(i, i ^ mask) for i in range(4)])


def after(array, other):
    return lax.optimization_barrier((array, other))


def on_device(queries, keys, values, cotangent):
    place = (lax.axis_index("z") * 4 + lax.axis_index("x")).reshape(1).astype(jnp.int32)
    mb = 1 << 20
    dma = pltpu.SemaphoreType.DMA
    half = shape(HEADS, 2, TOKENS_IN, DH)
    along_z = shape(8, 2, CHUNK, DH)
    first, second, block = shape(2, 352, DH), shape(2, 160, DH), shape(2, BLOCK, DH)
    own_rows, far_rows, edges = shape(2, 96, DH), shape(2, 640, DH), shape(2, 256, DH)
    pack = kernel_call(
        pack_body,
        [HBM] * 2,
        [(HBM, half)],
        scratch=[
            VMEM((2, TOKENS_IN, HEADS * DH), BF),
            VMEM((2, HEADS, TOKENS_IN, DH), BF),
            dma((2,)),
            dma((2,)),
        ],
        mib=LARGE,
        bytes_accessed=mb,
    )
    packed_kv = pack(keys, values)
    packed_qd = pack(queries, cotangent)
    kv, packed_qd = after(swap(packed_kv, HEAD_AXES), packed_qd)
    pyr, sent_z, p1, p2, p4 = kernel_call(
        pyramid_body,
        [SMEM, VMEM],
        [(VMEM, item) for item in (shape(2, 768, DH), along_z, edges, shape(2, 64, DH), block)],
        scratch=[VMEM((TOKENS, DH), F32)],
        bytes_accessed=2 * mb,
    )(place, kv)
    p4 = lax.ppermute(p4, SEQ_AXES, odd_pairs(RANKS))
    got_z = swap(sent_z, "z")
    packed_qd, got_z = after(packed_qd, got_z)
    own, p1, p2 = kernel_call(
        join_body, [SMEM] + [VMEM] * 3, [(VMEM, item) for item in (own_rows, first, second)]
    )(place, got_z, p1, p2)
    qd = swap(packed_qd, HEAD_AXES)
    far = kernel_call(
        merge_body, [SMEM] + [VMEM] * 5, [(VMEM, item) for item in (far_rows, edges)]
    )(place, own, flip(p1, 1), flip(p2, 2), flip(p2, 3), p4)
    out, dkv, *grads = kernel_call(
        attend_body,
        [SMEM] + [VMEM] * 5,
        [(VMEM, half), (VMEM, shape(2, TOKENS, DH, dtype=F32)), (VMEM, far_rows), (VMEM, edges)],
        scratch=[
            VMEM((2, 1280, DH), BF),
            VMEM((2, 1280, DH), F32),
            VMEM((2, 768, DH), F32),
            VMEM((2, 640, DH), F32),
            VMEM((TOKENS, DH), F32),
        ],
        mib=MIDDLE,
        flops=2 * 10**9,
        bytes_accessed=5 * mb,
    )(place, kv, qd, pyr, *far)
    small = shape(2, 64, DH)
    zx, b1, b2, b3, b4 = kernel_call(
        part_body,
        [SMEM] + [VMEM] * 2,
        [(VMEM, item) for item in (shape(RANKS, 2, CHUNK, DH), edges, small, small, block)],
    )(place, *grads)
    b1, b2, b3 = flip(b1, 1), flip(b2, 2), flip(b3, 3)
    b4 = lax.ppermute(b4, SEQ_AXES, odd_pairs(RANKS))
    packed = kernel_call(
        finish_body,
        [SMEM] + [VMEM] * 7,
        [(VMEM, shape(HEADS, 4, TOKENS_IN, DH))],
        scratch=[VMEM((TOKENS, DH), F32)],
        bytes_accessed=3 * mb,
    )(place, out, dkv, swap(zx, SEQ_AXES), b1, b2, b3, b4)
    results = swap(packed, HEAD_AXES)
    flat = shape(TOKENS_IN, HEADS * DH)
    return tuple(
        kernel_call(
            unpack_body,
            [VMEM],
            [(HBM, flat)] * 4,
            scratch=[VMEM((4, TOKENS_IN, HEADS * DH), BF), dma((4,))],
            bytes_accessed=2 * mb,
        )(results)
    )


def solution(mesh):
    fine = Mesh(mesh.devices.reshape(8, 4, 4, 2, 2), AXES)
    placed = P(AXES, None)
    return jax.shard_map(
        on_device,
        mesh=fine,
        in_specs=(placed,) * 4,
        out_specs=(placed,) * 4,
        check_vma=False,
    )
```
